32 devices in a mesh: dp: 8 (over z, y), rep: 4 (over x, core).
Axes of the slice: x: 2, y: 2, z: 4, core: 2. Of those that a mesh axis runs over, the one named last changes fastest.
Arguments:
- mentions: bfloat16 [4096, 1024], P(('dp', 'rep')), may hold values from -48 to 48
- entity_states: bfloat16 [4096, 1024], P(('dp', 'rep')), may hold values from -8 to 8
- head: bfloat16 [1024, 1024], P('dp'), may hold values from -4 to 4
Outputs:
- pair_loss: float32 [4096], P(('dp', 'rep'))
- mention_grad: bfloat16 [4096, 1024], P(('dp', 'rep'))
- state_grad: bfloat16 [4096, 1024], P(('dp', 'rep'))
The draws below stay inside these ranges and needn't reach their ends.
All inputs are finite; a program needn't handle non-finite values.
Results may differ from the reference program's by a relative error of at most 0.0073.
Values may be sent and summed in bfloat16 or wider, within the bound.
No kernel may reach another device: no remote copies, remote signals or barrier semaphores. Data moves between devices by JAX's collectives and lax.ppermute only.
A program may use at most 64 MiB of HBM per device.

```python
import math
import jax
import jax.numpy as jnp
from jax import lax

D = 1024
GROUP = 512
TOKENS = 4096


def entity_draw(key):
    base_states = jnp.clip(jax.random.normal(jax.random.fold_in(key, 11), (TOKENS, D), jnp.float32), -6.0, 6.0)
    return base_states


def draw_entity_states(key, part):
    return entity_draw(key).astype(jnp.bfloat16)


def draw_mentions(key, part):
    queries = jnp.clip(jax.random.normal(jax.random.fold_in(key, 21), (TOKENS, D), jnp.float32), -6.0, 6.0)
    return queries.astype(jnp.bfloat16)


def draw_head(key, part):
    noise = jnp.clip(jax.random.normal(jax.random.fold_in(key, 31), (D, D), jnp.float32), -6.0, 6.0)
    return (jnp.eye(D, dtype=jnp.float32) + 0.5 / math.sqrt(D) * noise).astype(jnp.bfloat16)


def setup_inputs(seed: int = 0) -> dict:
    streams_of = jax.random.split(jax.random.key(seed), 4)
    return {
        "mentions": draw_mentions(jax.random.fold_in(streams_of[3], 71), 0),
        "entity_states": draw_entity_states(jax.random.fold_in(streams_of[3], 71), 0),
        "head": draw_head(jax.random.fold_in(streams_of[3], 71), 0),
    }


def reference(mentions, entity_states, head):
    scale_factor = 3.0 / math.sqrt(D)
    projected = jnp.dot(entity_states, head, preferred_element_type=jnp.float32).astype(jnp.bfloat16)
    groups = TOKENS // GROUP
    mention_blocks = mentions.reshape(groups, GROUP, D)
    entity_blocks = projected.reshape(groups, GROUP, D)

    def per_group(operands):
        mention_blk, entity_blk = operands
        scores = jnp.dot(mention_blk, entity_blk.T, preferred_element_type=jnp.float32) * scale_factor
        row_max = lax.optimization_barrier(jnp.max(scores, axis=1))
        log_total = row_max + jnp.log(lax.optimization_barrier(jnp.sum(jnp.exp(scores - row_max[:, None]), axis=1)))
        chances = jnp.exp(scores - log_total[:, None]).astype(jnp.bfloat16)
        grad_m = scale_factor * (jnp.dot(chances, entity_blk, preferred_element_type=jnp.float32) - entity_blk.astype(jnp.float32))
        grad_e = scale_factor * (jnp.dot(chances.T, mention_blk, preferred_element_type=jnp.float32) - mention_blk.astype(jnp.float32))
        pair_loss = log_total - jnp.diagonal(scores)
        return (pair_loss, grad_m.astype(jnp.bfloat16), grad_e.astype(jnp.bfloat16))
    pair_loss, grad_m, grad_e = lax.map(per_group, (mention_blocks, entity_blocks))
    state_grad = jnp.dot(grad_e.reshape(TOKENS, D), head.T, preferred_element_type=jnp.float32).astype(jnp.bfloat16)
    return (pair_loss.reshape(TOKENS), grad_m.reshape(TOKENS, D), state_grad)
```

```python
import functools
import math

import jax
import jax.numpy as jnp
from jax import lax
from jax.experimental import pallas as pl
from jax.experimental.pallas import tpu as pltpu
from jax.sharding import PartitionSpec as P

LAST = (((1,), (1,)), ((), ()))
FIRST = (((0,), (0,)), ((), ()))


def dot(left, right, contract=(((1,), (0,)), ((), ()))):
    return lax.dot_general(left, right, contract, preferred_element_type=jnp.float32)


def kernel(dp, rep, scale, *refs):
    head_ref, refs = refs[0], refs[1:]
    mine_refs, refs = refs[: dp - 1], refs[dp - 1 :]
    theirs_refs, refs = refs[: dp - 1], refs[dp - 1 :]
    entity_refs, refs = refs[:rep], refs[rep:]
    mention_refs, refs = refs[:rep], refs[rep:]
    loss_ref, mention_grad_ref, state_grad_ref = refs[:3]
    head, entities, mentions, projected, sems = refs[3:]

    rows = entity_refs[0].shape[0]
    depth, half = head_ref.shape[0], mine_refs[0].shape[1]
    me, core = lax.axis_index("dp"), lax.rem(lax.axis_index("rep"), 2)

    copies = []

    def fetch(source, target):
        copy = pltpu.make_async_copy(source, target, sems.at[len(copies)])
        copy.start()
        copies.append(copy)

    def place(mask, column):
        at = pl.multiple_of(jnp.bitwise_xor(me, mask) * depth, depth)
        return head.at[pl.ds(at, depth), pl.ds(pl.multiple_of(column * half, half), half)]

    for i in range(rep):
        fetch(entity_refs[i], entities.at[pl.ds(i * rows, rows)])
    fetch(head_ref, head.at[pl.ds(pl.multiple_of(me * depth, depth), depth)])
    for mask in range(1, dp):
        fetch(mine_refs[mask - 1], place(mask, core))
        fetch(theirs_refs[mask - 1], place(mask, 1 - core))
    ready = len(copies)
    for i in range(rep):
        fetch(mention_refs[i], mentions.at[pl.ds(i * rows, rows)])

    for copy in copies[:ready]:
        copy.wait()
    group, width = projected.shape
    step = 256
    for at in range(0, width, step):
        projected[:, at : at + step] = dot(entities[...], head[:, at : at + step]).astype(jnp.bfloat16)
    for copy in copies[ready:]:
        copy.wait()

    block = min(group, 512)
    summed = jnp.zeros((rows, width), jnp.float32)
    for at in range(0, group, block):
        part = mentions[at : at + block, :]
        scores = dot(part, projected[...], LAST) * scale
        top = jnp.max(scores, axis=1, keepdims=True)
        powers = jnp.exp(scores - top)
        total = jnp.sum(powers, axis=1, keepdims=True)
        chances = (powers / total).astype(jnp.bfloat16)
        summed += dot(chances[:, :rows], part, FIRST)
        if at == 0:
            log_total = top[:rows] + jnp.log(total[:rows])
            eye = lax.broadcasted_iota(jnp.int32, (rows, rows), 0) == lax.broadcasted_iota(
                jnp.int32, (rows, rows), 1
            )
            losses = jnp.where(eye, log_total - scores[:rows, :rows], 0.0)
            loss_ref[...] = jnp.sum(losses, axis=0)
            weighted = dot(chances[:rows], projected[...])
            mention_grad_ref[...] = (
                scale * (weighted - projected[:rows, :].astype(jnp.float32))
            ).astype(jnp.bfloat16)
    proj_grad = (scale * (summed - mentions[:rows, :].astype(jnp.float32))).astype(jnp.bfloat16)
    state_grad_ref[...] = dot(proj_grad, head[...], LAST).astype(jnp.bfloat16)


def solution(mesh):
    dp, rep = mesh.shape["dp"], mesh.shape["rep"]

    def send(x, over_dp, over_rep):
        pairs = [
            (d * rep + r, (d ^ over_dp) * rep + (r ^ over_rep)) for d in range(dp) for r in range(rep)
        ]
        return lax.ppermute(x, ("dp", "rep"), pairs)

    def local(mentions, entity_states, head):
        rows, width = mentions.shape
        half = width // 2
        core = lax.rem(lax.axis_index("rep"), 2)
        own = lax.dynamic_slice_in_dim(head, core * half, half, axis=1)

        mine = {}
        for mask in range(2, dp, 2):
            mine[mask] = send(own, mask, 0)
        mine[1] = send(own, 1, 0)
        entities, held = {0: entity_states}, {0: mentions}
        for store in (entities, held):
            for mask in range(2, rep, 2):
                store[mask] = send(store[0], 0, mask)
            for mask in range(0, rep, 2):
                store[mask + 1] = send(store[mask], 0, 1)
        for mask in range(2, dp, 2):
            mine[mask + 1] = send(mine[mask], 1, 0)
        theirs = {mask: send(mine[mask], 0, 1) for mask in range(1, dp)}

        operands = (
            [head]
            + [mine[i] for i in range(1, dp)]
            + [theirs[i] for i in range(1, dp)]
            + [entities[i] for i in range(rep)]
            + [held[i] for i in range(rep)]
        )
        group = rep * rows
        anywhere = pl.BlockSpec(memory_space=pl.ANY)
        vmem = pl.BlockSpec(memory_space=pltpu.VMEM)
        return pl.pallas_call(
            functools.partial(kernel, dp, rep, 3.0 / math.sqrt(width)),
            out_shape=(
                jax.ShapeDtypeStruct((rows,), jnp.float32),
                jax.ShapeDtypeStruct((rows, width), jnp.bfloat16),
                jax.ShapeDtypeStruct((rows, width), jnp.bfloat16),
            ),
            in_specs=[anywhere] * len(operands),
            out_specs=(vmem, vmem, vmem),
            scratch_shapes=[
                pltpu.VMEM((dp * head.shape[0], width), jnp.bfloat16),
                pltpu.VMEM((group, width), jnp.bfloat16),
                pltpu.VMEM((group, width), jnp.bfloat16),
                pltpu.VMEM((group, width), jnp.bfloat16),
                pltpu.SemaphoreType.DMA((len(operands),)),
            ],
            compiler_params=pltpu.CompilerParams(vmem_limit_bytes=48 * 1024 * 1024),
            name="group_softmax",
        )(*operands)

    return jax.shard_map(
        local,
        mesh=mesh,
        in_specs=(P(("dp", "rep"), None), P(("dp", "rep"), None), P("dp", None)),
        out_specs=(P(("dp", "rep")), P(("dp", "rep"), None), P(("dp", "rep"), None)),
        check_vma=False,
    )
```

```python
import functools
import math

import jax
import jax.numpy as jnp
from jax import lax
from jax.experimental import pallas as pl
from jax.experimental.pallas import tpu as pltpu
from jax.sharding import PartitionSpec as P

LAST = (((1,), (1,)), ((), ()))
FIRST = (((0,), (0,)), ((), ()))


def dot(left, right, contract=(((1,), (0,)), ((), ()))):
    return lax.dot_general(left, right, contract, preferred_element_type=jnp.float32)


def kernel(dp, rep, scale, slots, *refs):
    head_ref, refs = refs[0], refs[1:]
    pieces, refs = refs[: 2 * len(slots)], refs[2 * len(slots) :]
    entity_refs, refs = refs[:rep], refs[rep:]
    mention_refs, refs = refs[:rep], refs[rep:]
    loss_ref, mention_grad_ref, state_grad_ref = refs[:3]
    head, entities, mentions, projected, sems = refs[3:]

    rows = entity_refs[0].shape[0]
    depth = head_ref.shape[0]
    me, core = lax.axis_index("dp"), lax.rem(lax.axis_index("rep"), 2)

    copies = []

    def fetch(source, target):
        copy = pltpu.make_async_copy(source, target, sems.at[len(copies)])
        copy.start()
        copies.append(copy)

    def place(mask):
        at = pl.multiple_of(jnp.bitwise_xor(me, mask) * depth, depth)
        return head.at[pl.ds(at, depth)]

    for i in range(rep):
        fetch(entity_refs[i], entities.at[pl.ds(i * rows, rows)])
    fetch(head_ref, place(0))
    for i, (_, _, masks) in enumerate(slots):
        near, other = pieces[2 * i : 2 * i + 2]
        if masks[1] is None:
            copy = pltpu.make_async_copy(near, place(masks[0]), sems.at[len(copies)])
            pl.when(core == 0)(copy.start)
            pl.when(core == 1)(pltpu.make_async_copy(other, place(masks[0]), sems.at[len(copies)]).start)
            copies.append(copy)
        else:
            fetch(near, place(jnp.where(core == 0, *masks)))
            fetch(other, place(jnp.where(core == 0, *masks[::-1])))
    ready = len(copies)
    for i in range(rep):
        fetch(mention_refs[i], mentions.at[pl.ds(i * rows, rows)])

    for copy in copies[:ready]:
        copy.wait()
    group, width = projected.shape
    step = 256
    for at in range(0, width, step):
        projected[:, at : at + step] = dot(entities[...], head[:, at : at + step]).astype(jnp.bfloat16)
    for copy in copies[ready:]:
        copy.wait()

    block = min(group, 512)
    summed = jnp.zeros((rows, width), jnp.float32)
    for at in range(0, group, block):
        part = mentions[at : at + block, :]
        scores = dot(part, projected[...], LAST) * scale
        top = jnp.max(scores, axis=1, keepdims=True)
        powers = jnp.exp(scores - top)
        total = jnp.sum(powers, axis=1, keepdims=True)
        chances = (powers / total).astype(jnp.bfloat16)
        summed += dot(chances[:, :rows], part, FIRST)
        if at == 0:
            log_total = top[:rows] + jnp.log(total[:rows])
            eye = lax.broadcasted_iota(jnp.int32, (rows, rows), 0) == lax.broadcasted_iota(
                jnp.int32, (rows, rows), 1
            )
            losses = jnp.where(eye, log_total - scores[:rows, :rows], 0.0)
            loss_ref[...] = jnp.sum(losses, axis=0)
            weighted = dot(chances[:rows], projected[...])
            mention_grad_ref[...] = (
                scale * (weighted - projected[:rows, :].astype(jnp.float32))
            ).astype(jnp.bfloat16)
    proj_grad = (scale * (summed - mentions[:rows, :].astype(jnp.float32))).astype(jnp.bfloat16)
    state_grad_ref[...] = dot(proj_grad, head[...], LAST).astype(jnp.bfloat16)


def plan(dp):
    children = {mask: [] for mask in range(dp)}
    for mask in range(1, dp):
        step = mask & -mask
        children[0 if mask in (step, dp - 1) else mask ^ step].append(mask)
    first = sorted(children[0], key=lambda m: (-len(children[m]), -m))
    slots = [(-1, masks, masks) for masks in zip(first[::2], first[1::2] + [None] * (len(first) % 2))]
    for i, (_, _, held) in enumerate(slots):
        lists = [[] if m is None else children[m] for m in held]
        for j in range(max(map(len, lists))):
            masks = tuple(own[j] if j < len(own) else None for own in lists)
            steps = tuple(None if m is None else m ^ h for m, h in zip(masks, held))
            slots.append((i, steps, masks))
    return slots


def solution(mesh):
    dp, rep = mesh.shape["dp"], mesh.shape["rep"]

    slots = plan(dp)

    def send(x, over_dp, over_rep=0):
        pairs = [
            (d * rep + r, (d ^ over_dp[r % 2]) * rep + (r ^ over_rep))
            for d in range(dp)
            for r in range(rep)
            if over_dp[r % 2] is not None
        ]
        return lax.ppermute(x, ("dp", "rep"), pairs)

    def after(x, done):
        return lax.optimization_barrier((x, done))[0]

    def local(mentions, entity_states, head):
        rows, width = mentions.shape
        entities, held = {0: entity_states}, {0: mentions}
        for store in (entities, held):
            for mask in range(2, rep, 2):
                store[mask] = send(store[0], (0, 0), mask)
        entities[1] = send(entities[0], (0, 0), 1)
        pieces = []
        for i, (source, steps, masks) in enumerate(slots):
            start = head if i == 0 else after(head, entities[1])
            near = send(start if source < 0 else pieces[2 * source], steps)
            pieces += [near, send(near, [None if m is None else 0 for m in masks], 1)]
        held[1] = send(after(held[0], pieces[0]), (0, 0), 1)
        for store in (entities, held):
            for mask in range(2, rep, 2):
                store[mask + 1] = send(after(store[mask], pieces[0]), (0, 0), 1)

        head, entities[0], held[0] = (pltpu.with_memory_space_constraint(x, pltpu.HBM) for x in (head, entities[0], held[0]))
        operands = [head] + pieces + [entities[i] for i in range(rep)] + [held[i] for i in range(rep)]
        group = rep * rows
        anywhere = pl.BlockSpec(memory_space=pl.ANY)
        vmem = pl.BlockSpec(memory_space=pltpu.VMEM)
        return pl.pallas_call(
            functools.partial(kernel, dp, rep, 3.0 / math.sqrt(width), slots),
            out_shape=(
                jax.ShapeDtypeStruct((rows,), jnp.float32),
                jax.ShapeDtypeStruct((rows, width), jnp.bfloat16),
                jax.ShapeDtypeStruct((rows, width), jnp.bfloat16),
            ),
            in_specs=[anywhere] * len(operands),
            out_specs=(vmem, vmem, vmem),
            scratch_shapes=[
                pltpu.VMEM((dp * head.shape[0], width), jnp.bfloat16),
                pltpu.VMEM((group, width), jnp.bfloat16),
                pltpu.VMEM((group, width), jnp.bfloat16),
                pltpu.VMEM((group, width), jnp.bfloat16),
                pltpu.SemaphoreType.DMA((len(operands),)),
            ],
            compiler_params=pltpu.CompilerParams(vmem_limit_bytes=48 * 1024 * 1024),
            name="group_softmax",
        )(*operands)

    return jax.shard_map(
        local,
        mesh=mesh,
        in_specs=(P(("dp", "rep"), None), P(("dp", "rep"), None), P("dp", None)),
        out_specs=(P(("dp", "rep")), P(("dp", "rep"), None), P(("dp", "rep"), None)),
        check_vma=False,
    )
```

```python
import functools
import math

import jax
import jax.numpy as jnp
from jax import lax
from jax.experimental import pallas as pl
from jax.experimental.pallas import tpu as pltpu
from jax.sharding import PartitionSpec as P

BLOCK = 512
LAST, FIRST = ((1,), (1,)), ((0,), (0,))


def dot(left, right, contract=((1,), (0,))):
    return lax.dot_general(left, right, (contract, ((), ())), preferred_element_type=jnp.float32)


def plan(dp):
    if dp == 8:
        return [(-1, (4, 2), (4, 2)), (-1, (0, 1), (0, 1)), (0, (1, 5), (5, 7)), (0, (2, 1), (6, 3))]
    return [(-1, (m, m + 1), (m, m + 1)) for m in range(0, dp, 2)]


def kernel(dp, rep, scale, slots, *refs):
    head_ref, refs = refs[0], refs[1:]
    pieces, refs = refs[: 2 * len(slots)], refs[2 * len(slots) :]
    entity_refs, refs = refs[:rep], refs[rep:]
    mention_refs, refs = refs[:rep], refs[rep:]
    loss_ref, mention_grad_ref, state_grad_ref = refs[:3]
    head, entities, mentions, projected, sems = refs[3:]

    rows, depth = entity_refs[0].shape[0], head_ref.shape[0]
    me, core = lax.axis_index("dp"), lax.rem(lax.axis_index("rep"), 2)

    copies = []

    def place(mask):
        at = pl.multiple_of(jnp.bitwise_xor(me, mask) * depth, depth)
        return head.at[pl.ds(at, depth)]

    def fetch(source, target):
        copies.append(pltpu.make_async_copy(source, target, sems.at[len(copies)]))
        copies[-1].start()

    for i in range(rep):
        fetch(entity_refs[i], entities.at[pl.ds(i * rows, rows)])
    fetch(head_ref, place(0))
    for i, (_, _, masks) in enumerate(slots):
        near, other = pieces[2 * i : 2 * i + 2]
        if masks[0] == 0:
            copies.append(pltpu.make_async_copy(near, place(masks[1]), sems.at[len(copies)]))
            pl.when(core == 1)(copies[-1].start)
            swapped = pltpu.make_async_copy(other, place(masks[1]), sems.at[len(copies) - 1])
            pl.when(core == 0)(swapped.start)
        else:
            fetch(near, place(jnp.where(core == 0, *masks)))
            fetch(other, place(jnp.where(core == 0, *masks[::-1])))
    ready = len(copies)
    for i in range(rep):
        fetch(mention_refs[i], mentions.at[pl.ds(i * rows, rows)])

    for copy in copies[:ready]:
        copy.wait()
    group, width = projected.shape
    step = min(width, 256)
    for at in range(0, width, step):
        projected[:, at : at + step] = dot(entities[...], head[:, at : at + step]).astype(jnp.bfloat16)
    for copy in copies[ready:]:
        copy.wait()

    block = min(group, BLOCK)
    summed = jnp.zeros((rows, width), jnp.float32)
    for at in range(0, group, block):
        part = mentions[at : at + block, :]
        scores = dot(part, projected[...], LAST) * scale
        top = jnp.max(scores, axis=1, keepdims=True)
        powers = jnp.exp(scores - top)
        total = jnp.sum(powers, axis=1, keepdims=True)
        chances = (powers / total).astype(jnp.bfloat16)
        summed += dot(chances[:, :rows], part, FIRST)
        if at == 0:
            log_total = top[:rows] + jnp.log(total[:rows])
            eye = lax.broadcasted_iota(jnp.int32, (rows, rows), 0) == lax.broadcasted_iota(
                jnp.int32, (rows, rows), 1
            )
            loss_ref[...] = jnp.sum(jnp.where(eye, log_total - scores[:rows, :rows], 0.0), axis=0)
            weighted = dot(chances[:rows], projected[...])
            mention_grad_ref[...] = (
                scale * (weighted - projected[:rows, :].astype(jnp.float32))
            ).astype(jnp.bfloat16)
    proj_grad = (scale * (summed - mentions[:rows, :].astype(jnp.float32))).astype(jnp.bfloat16)
    state_grad_ref[...] = dot(proj_grad, head[...], LAST).astype(jnp.bfloat16)


def solution(mesh):
    dp, rep = mesh.shape["dp"], mesh.shape["rep"]
    slots = plan(dp)

    def send(x, over_dp=(0, 0), over_rep=0):
        pairs = [
            (d * rep + r, (d ^ over_dp[r % 2]) * rep + (r ^ over_rep)) for d in range(dp) for r in range(rep)
        ]
        return lax.ppermute(x, ("dp", "rep"), pairs)

    def local(mentions, entity_states, head):
        rows, width = mentions.shape
        group = rep * rows
        entities, held = {0: entity_states}, {0: mentions}
        for store in (entities, held):
            store[1] = send(store[0], over_rep=1)
            for mask in range(2, rep, 2):
                store[mask] = send(store[0], over_rep=mask)
                store[mask + 1] = send(store[mask], over_rep=1)
        pieces = []
        for source, steps, _ in slots:
            near = send(head if source < 0 else pieces[2 * source], steps)
            pieces += [near, send(near, over_rep=1)]

        head, entities[0], held[0] = (
            pltpu.with_memory_space_constraint(x, pltpu.HBM) for x in (head, entities[0], held[0])
        )
        operands = [head] + pieces + [entities[i] for i in range(rep)] + [held[i] for i in range(rep)]
        anywhere = pl.BlockSpec(memory_space=pl.ANY)
        vmem = pl.BlockSpec(memory_space=pltpu.VMEM)
        return pl.pallas_call(
            functools.partial(kernel, dp, rep, 3.0 / math.sqrt(width), slots),
            out_shape=(
                jax.ShapeDtypeStruct((rows,), jnp.float32),
                jax.ShapeDtypeStruct((rows, width), jnp.bfloat16),
                jax.ShapeDtypeStruct((rows, width), jnp.bfloat16),
            ),
            in_specs=[anywhere] * len(operands),
            out_specs=(vmem, vmem, vmem),
            scratch_shapes=[
                pltpu.VMEM((dp * head.shape[0], width), jnp.bfloat16),
                pltpu.VMEM((group, width), jnp.bfloat16),
                pltpu.VMEM((group, width), jnp.bfloat16),
                pltpu.VMEM((group, width), jnp.bfloat16),
                pltpu.SemaphoreType.DMA((len(operands),)),
            ],
            compiler_params=pltpu.CompilerParams(vmem_limit_bytes=40 * 1024 * 1024),
            name="group_softmax",
        )(*operands)

    return jax.shard_map(
        local,
        mesh=mesh,
        in_specs=(P(("dp", "rep"), None), P(("dp", "rep"), None), P("dp", None)),
        out_specs=(P(("dp", "rep")), P(("dp", "rep"), None), P(("dp", "rep"), None)),
        check_vma=False,
    )
```

```python
import functools
import math

import jax
import jax.numpy as jnp
from jax import lax
from jax.experimental import pallas as pl
from jax.experimental.pallas import tpu as pltpu
from jax.sharding import PartitionSpec as P

BLOCK = 512
LAST, FIRST = ((1,), (1,)), ((0,), (0,))


def dot(left, right, contract=((1,), (0,))):
    return lax.dot_general(left, right, (contract, ((), ())), preferred_element_type=jnp.float32)


def plan(dp):
    if dp == 8:
        return [(-1, (4, 2), (4, 2)), (-1, (0, 1), (0, 1)), (0, (1, 5), (5, 7)), (0, (2, 1), (6, 3))]
    return [(-1, (m, m + 1), (m, m + 1)) for m in range(0, dp, 2)]


def kernel(dp, rep, scale, slots, *refs):
    pieces, refs = refs[1 : 2 * len(slots) + 1], refs[2 * len(slots) + 1 :]
    entity_refs, refs = refs[:rep], refs[rep:]
    mention_refs, refs = refs[:rep], refs[rep:]
    loss_ref, mention_grad_ref, state_grad_ref = refs[:3]
    head, entities, mentions, projected, sems = refs[3:]

    rows, depth = entity_refs[0].shape[0], pieces[0].shape[0]
    me, core = lax.axis_index("dp"), lax.rem(lax.axis_index("rep"), 2)

    copies = []

    def place(mask):
        at = pl.multiple_of(jnp.bitwise_xor(me, mask) * depth, depth)
        return head.at[pl.ds(at, depth)]

    def fetch(source, target):
        copies.append(pltpu.make_async_copy(source, target, sems.at[len(copies)]))
        copies[-1].start()

    fetch(entity_refs[0], entities.at[pl.ds(0, rows)])
    fetch(mention_refs[0], mentions.at[pl.ds(0, rows)])
    for i in range(1, rep):
        fetch(entity_refs[i], entities.at[pl.ds(i * rows, rows)])
    for i, (_, _, masks) in enumerate(slots):
        fetch(pieces[2 * i], place(jnp.where(core == 0, *masks)))
        fetch(pieces[2 * i + 1], place(jnp.where(core == 0, *masks[::-1])))
    ready = len(copies)
    for i in range(1, rep):
        fetch(mention_refs[i], mentions.at[pl.ds(i * rows, rows)])

    for copy in copies[2:ready]:
        copy.wait()
    group, width = projected.shape
    step = min(width, 256)
    for to in (slice(rows, group), slice(0, rows)):
        if to.start == 0:
            copies[0].wait()
        for at in range(0, width, step):
            projected[to, at : at + step] = dot(entities[to, :], head[:, at : at + step]).astype(jnp.bfloat16)
    copies[1].wait()
    for copy in copies[ready:]:
        copy.wait()

    block = min(group, BLOCK)
    summed = jnp.zeros((rows, width), jnp.float32)
    for at in range(0, group, block):
        part = mentions[at : at + block, :]
        scores = dot(part, projected[...], LAST) * scale
        top = jnp.max(scores, axis=1, keepdims=True)
        powers = jnp.exp(scores - top)
        total = jnp.sum(powers, axis=1, keepdims=True)
        chances = (powers / total).astype(jnp.bfloat16)
        summed += dot(chances[:, :rows], part, FIRST)
        if at == 0:
            log_total = top[:rows] + jnp.log(total[:rows])
            eye = lax.broadcasted_iota(jnp.int32, (rows, rows), 0) == lax.broadcasted_iota(
                jnp.int32, (rows, rows), 1
            )
            loss_ref[...] = jnp.sum(jnp.where(eye, log_total - scores[:rows, :rows], 0.0), axis=0)
            weighted = dot(chances[:rows], projected[...])
            mention_grad_ref[...] = (
                scale * (weighted - projected[:rows, :].astype(jnp.float32))
            ).astype(jnp.bfloat16)
    proj_grad = (scale * (summed - mentions[:rows, :].astype(jnp.float32))).astype(jnp.bfloat16)
    state_grad_ref[...] = dot(proj_grad, head[...], LAST).astype(jnp.bfloat16)


def solution(mesh):
    dp, rep = mesh.shape["dp"], mesh.shape["rep"]
    slots = plan(dp)

    def send(x, over_dp=(0, 0), over_rep=0):
        pairs = [
            (d * rep + r, (d ^ over_dp[r % 2]) * rep + (r ^ over_rep)) for d in range(dp) for r in range(rep)
        ]
        return lax.ppermute(x, ("dp", "rep"), pairs)

    def local(mentions, entity_states, head):
        rows, width = mentions.shape
        group = rep * rows
        entities, held = {0: entity_states}, {0: mentions}
        for store in (entities, held):
            store[1] = send(store[0], over_rep=1)
            for mask in range(2, rep, 2):
                store[mask] = send(store[0], over_rep=mask)
                store[mask + 1] = send(store[mask], over_rep=1)
        pieces = []
        for source, steps, _ in slots:
            near = send(head if source < 0 else pieces[2 * source], steps)
            pieces += [near, send(near, over_rep=1)]

        head, entities[0], held[0] = (
            pltpu.with_memory_space_constraint(x, pltpu.HBM) for x in (head, entities[0], held[0])
        )
        operands = [head] + pieces + [entities[i] for i in range(rep)] + [held[i] for i in range(rep)]
        anywhere = pl.BlockSpec(memory_space=pl.ANY)
        vmem = pl.BlockSpec(memory_space=pltpu.VMEM)
        return pl.pallas_call(
            functools.partial(kernel, dp, rep, 3.0 / math.sqrt(width), slots),
            out_shape=(
                jax.ShapeDtypeStruct((rows,), jnp.float32),
                jax.ShapeDtypeStruct((rows, width), jnp.bfloat16),
                jax.ShapeDtypeStruct((rows, width), jnp.bfloat16),
            ),
            in_specs=[anywhere] * len(operands),
            out_specs=(vmem, vmem, vmem),
            scratch_shapes=[
                pltpu.VMEM((dp * head.shape[0], width), jnp.bfloat16),
                pltpu.VMEM((group, width), jnp.bfloat16),
                pltpu.VMEM((group, width), jnp.bfloat16),
                pltpu.VMEM((group, width), jnp.bfloat16),
                pltpu.SemaphoreType.DMA((len(operands),)),
            ],
            compiler_params=pltpu.CompilerParams(vmem_limit_bytes=40 * 1024 * 1024),
            name="group_softmax",
        )(*operands)

    return jax.shard_map(
        local,
        mesh=mesh,
        in_specs=(P(("dp", "rep"), None), P(("dp", "rep"), None), P("dp", None)),
        out_specs=(P(("dp", "rep")), P(("dp", "rep"), None), P(("dp", "rep"), None)),
        check_vma=False,
    )
```

```python
import functools
import math

import jax
import jax.numpy as jnp
from jax import lax
from jax.experimental import pallas as pl
from jax.experimental.pallas import tpu as pltpu
from jax.sharding import PartitionSpec as P

BLOCK = 512
LAST, FIRST = ((1,), (1,)), ((0,), (0,))


def dot(left, right, contract=((1,), (0,))):
    return lax.dot_general(left, right, (contract, ((), ())), preferred_element_type=jnp.float32)


def plan(dp):
    if dp == 8:
        return [(-1, (4, 2), (4, 2)), (-1, (0, 1), (0, 1)), (0, (1, 5), (5, 7)), (0, (2, 1), (6, 3))]
    return [(-1, (m, m + 1), (m, m + 1)) for m in range(0, dp, 2)]


def kernel(dp, rep, scale, slots, *refs):
    pieces, refs = refs[1 : 2 * len(slots) + 1], refs[2 * len(slots) + 1 :]
    entity_refs, refs = refs[:rep], refs[rep:]
    mention_refs, refs = refs[:rep], refs[rep:]
    loss_ref, mention_grad_ref, state_grad_ref = refs[:3]
    head, entities, mentions, projected, sems = refs[3:]

    rows, depth = entity_refs[0].shape[0], pieces[0].shape[0]
    me, core = lax.axis_index("dp"), lax.rem(lax.axis_index("rep"), 2)

    copies = []

    def place(mask):
        at = pl.multiple_of(jnp.bitwise_xor(me, mask) * depth, depth)
        return head.at[pl.ds(at, depth)]

    def fetch(source, target):
        copies.append(pltpu.make_async_copy(source, target, sems.at[len(copies)]))
        copies[-1].start()

    fetch(entity_refs[0], entities.at[pl.ds(0, rows)])
    fetch(mention_refs[0], mentions.at[pl.ds(0, rows)])
    for i, (_, _, masks) in enumerate(slots):
        fetch(pieces[2 * i], place(jnp.where(core == 0, *masks)))
        fetch(pieces[2 * i + 1], place(jnp.where(core == 0, *masks[::-1])))
    ready = len(copies)
    for i in range(1, rep):
        fetch(mention_refs[i], mentions.at[pl.ds(i * rows, rows)])

    for copy in copies[2:ready]:
        copy.wait()
    group, width = projected.shape
    step = min(width, 512)
    for to in (slice(rows, group), slice(0, rows)):
        if to.start == 0:
            copies[0].wait()
        for at in range(0, width, step):
            part = entities[...] if to.start == 0 else jnp.concatenate([ref[...] for ref in entity_refs[1:]], axis=0)
            projected[to, at : at + step] = dot(part, head[:, at : at + step]).astype(jnp.bfloat16)
    copies[1].wait()
    for copy in copies[ready:]:
        copy.wait()

    block = min(group, BLOCK)
    summed = jnp.zeros((rows, width), jnp.float32)
    for at in range(0, group, block):
        part = mentions[at : at + block, :]
        scores = dot(part, projected[...], LAST) * scale
        top = jnp.max(scores, axis=1, keepdims=True)
        powers = jnp.exp(scores - top)
        total = jnp.sum(powers, axis=1, keepdims=True)
        chances = (powers / total).astype(jnp.bfloat16)
        summed += dot(chances[:, :rows], part, FIRST)
        if at == 0:
            log_total = top[:rows] + jnp.log(total[:rows])
            eye = lax.broadcasted_iota(jnp.int32, (rows, rows), 0) == lax.broadcasted_iota(
                jnp.int32, (rows, rows), 1
            )
            loss_ref[...] = jnp.sum(jnp.where(eye, log_total - scores[:rows, :rows], 0.0), axis=0)
            weighted = dot(chances[:rows], projected[...])
            mention_grad_ref[...] = (
                scale * (weighted - projected[:rows, :].astype(jnp.float32))
            ).astype(jnp.bfloat16)
    proj_grad = (scale * (summed - mentions[:rows, :].astype(jnp.float32))).astype(jnp.bfloat16)
    state_grad_ref[...] = dot(proj_grad, head[...], LAST).astype(jnp.bfloat16)


def solution(mesh):
    dp, rep = mesh.shape["dp"], mesh.shape["rep"]
    slots = plan(dp)

    def send(x, over_dp=(0, 0), over_rep=0):
        pairs = [
            (d * rep + r, (d ^ over_dp[r % 2]) * rep + (r ^ over_rep)) for d in range(dp) for r in range(rep)
        ]
        return lax.ppermute(x, ("dp", "rep"), pairs)

    def local(mentions, entity_states, head):
        rows, width = mentions.shape
        group = rep * rows
        entities, held = {0: entity_states}, {0: mentions}
        for store in (entities, held):
            store[1] = send(store[0], over_rep=1)
            for mask in range(2, rep, 2):
                store[mask] = send(store[0], over_rep=mask)
                store[mask + 1] = send(store[mask], over_rep=1)
        pieces = []
        for source, steps, _ in slots:
            near = send(head if source < 0 else pieces[2 * source], steps)
            pieces += [near, send(near, over_rep=1)]

        head, entities[0], held[0] = (
            pltpu.with_memory_space_constraint(x, pltpu.HBM) for x in (head, entities[0], held[0])
        )
        operands = [head] + pieces + [entities[i] for i in range(rep)] + [held[i] for i in range(rep)]
        anywhere = pl.BlockSpec(memory_space=pl.ANY)
        vmem = pl.BlockSpec(memory_space=pltpu.VMEM)
        return pl.pallas_call(
            functools.partial(kernel, dp, rep, 3.0 / math.sqrt(width), slots),
            out_shape=(
                jax.ShapeDtypeStruct((rows,), jnp.float32),
                jax.ShapeDtypeStruct((rows, width), jnp.bfloat16),
                jax.ShapeDtypeStruct((rows, width), jnp.bfloat16),
            ),
            in_specs=[anywhere] * (len(pieces) + 2) + [vmem] * (rep - 1) + [anywhere] * rep,
            out_specs=(vmem, vmem, vmem),
            scratch_shapes=[
                pltpu.VMEM((dp * head.shape[0], width), jnp.bfloat16),
                pltpu.VMEM((rows, width), jnp.bfloat16),
                pltpu.VMEM((group, width), jnp.bfloat16),
                pltpu.VMEM((group, width), jnp.bfloat16),
                pltpu.SemaphoreType.DMA((len(operands),)),
            ],
            compiler_params=pltpu.CompilerParams(vmem_limit_bytes=40 * 1024 * 1024),
            name="group_softmax",
        )(*operands)

    return jax.shard_map(
        local,
        mesh=mesh,
        in_specs=(P(("dp", "rep"), None), P(("dp", "rep"), None), P("dp", None)),
        out_specs=(P(("dp", "rep")), P(("dp", "rep"), None), P(("dp", "rep"), None)),
        check_vma=False,
    )
```

```python
import functools
import math

import jax
import jax.numpy as jnp
from jax import lax
from jax.experimental import pallas as pl
from jax.experimental.pallas import tpu as pltpu
from jax.sharding import PartitionSpec as P

BLOCK = 512
LAST, FIRST = ((1,), (1,)), ((0,), (0,))


def dot(left, right, contract=((1,), (0,))):
    return lax.dot_general(left, right, (contract, ((), ())), preferred_element_type=jnp.float32)


def plan(dp):
    if dp == 8:
        return [(-1, (4, 2), (4, 2)), (-1, (0, 1), (0, 1)), (0, (1, 5), (5, 7)), (0, (2, 1), (6, 3))]
    return [(-1, (m, m + 1), (m, m + 1)) for m in range(0, dp, 2)]


def kernel(dp, rep, scale, slots, *refs):
    pieces, refs = refs[1 : 2 * len(slots) + 1], refs[2 * len(slots) + 1 :]
    entity_refs, refs = refs[:rep], refs[rep:]
    mention_refs, refs = refs[:rep], refs[rep:]
    loss_ref, mention_grad_ref, state_grad_ref = refs[:3]
    head, entities, mentions, projected, sems = refs[3:]

    rows, depth = entity_refs[0].shape[0], pieces[0].shape[0]
    me, core = lax.axis_index("dp"), lax.rem(lax.axis_index("rep"), 2)

    copies = []

    def place(mask):
        at = pl.multiple_of(jnp.bitwise_xor(me, mask) * depth, depth)
        return head.at[pl.ds(at, depth)]

    def fetch(source, target):
        copies.append(pltpu.make_async_copy(source, target, sems.at[len(copies)]))
        copies[-1].start()

    fetch(entity_refs[0], entities.at[pl.ds(0, rows)])
    fetch(mention_refs[0], mentions.at[pl.ds(0, rows)])
    for i in range(1, rep):
        fetch(entity_refs[i], entities.at[pl.ds(i * rows, rows)])
    for i, (_, _, masks) in enumerate(slots):
        fetch(pieces[2 * i], place(jnp.where(core == 0, *masks)))
        fetch(pieces[2 * i + 1], place(jnp.where(core == 0, *masks[::-1])))
    ready = len(copies)
    for i in range(1, rep):
        fetch(mention_refs[i], mentions.at[pl.ds(i * rows, rows)])

    for copy in copies[2:ready]:
        copy.wait()
    group, width = projected.shape
    step = min(width, 512)
    for to in (slice(rows, group), slice(0, rows)):
        if to.start == 0:
            copies[0].wait()
        for at in range(0, width, step):
            projected[to, at : at + step] = dot(entities[to, :], head[:, at : at + step]).astype(jnp.bfloat16)
    copies[1].wait()
    for copy in copies[ready:]:
        copy.wait()

    block = min(group, BLOCK)
    summed = jnp.zeros((rows, width), jnp.float32)
    for at in range(0, group, block):
        part = mentions[at : at + block, :]
        scores = dot(part, projected[...], LAST) * scale
        top = jnp.max(scores, axis=1, keepdims=True)
        powers = jnp.exp(scores - top)
        total = jnp.sum(powers, axis=1, keepdims=True)
        chances = (powers / total).astype(jnp.bfloat16)
        summed += dot(chances[:, :rows], part, FIRST)
        if at == 0:
            log_total = top[:rows] + jnp.log(total[:rows])
            eye = lax.broadcasted_iota(jnp.int32, (rows, rows), 0) == lax.broadcasted_iota(
                jnp.int32, (rows, rows), 1
            )
            loss_ref[...] = jnp.sum(jnp.where(eye, log_total - scores[:rows, :rows], 0.0), axis=0)
            weighted = dot(chances[:rows], projected[...])
            mention_grad_ref[...] = (
                scale * (weighted - projected[:rows, :].astype(jnp.float32))
            ).astype(jnp.bfloat16)
    proj_grad = (scale * (summed - mentions[:rows, :].astype(jnp.float32))).astype(jnp.bfloat16)
    state_grad_ref[...] = dot(proj_grad, head[...], LAST).astype(jnp.bfloat16)


def solution(mesh):
    dp, rep = mesh.shape["dp"], mesh.shape["rep"]
    slots = plan(dp)

    def send(x, over_dp=(0, 0), over_rep=0):
        pairs = [
            (d * rep + r, (d ^ over_dp[r % 2]) * rep + (r ^ over_rep)) for d in range(dp) for r in range(rep)
        ]
        return lax.ppermute(x, ("dp", "rep"), pairs)

    def local(mentions, entity_states, head):
        rows, width = mentions.shape
        group = rep * rows
        entities, held = {0: entity_states}, {0: mentions}
        for store in (entities, held):
            store[1] = send(store[0], over_rep=1)
            for mask in range(2, rep, 2):
                store[mask] = send(store[0], over_rep=mask)
                store[mask + 1] = send(store[mask], over_rep=1)
        pieces = []
        for source, steps, _ in slots:
            near = send(head if source < 0 else pieces[2 * source], steps)
            pieces += [near, send(near, over_rep=1)]

        head, entities[0], held[0] = (
            pltpu.with_memory_space_constraint(x, pltpu.HBM) for x in (head, entities[0], held[0])
        )
        operands = [head] + pieces + [entities[i] for i in range(rep)] + [held[i] for i in range(rep)]
        anywhere = pl.BlockSpec(memory_space=pl.ANY)
        vmem = pl.BlockSpec(memory_space=pltpu.VMEM)
        return pl.pallas_call(
            functools.partial(kernel, dp, rep, 3.0 / math.sqrt(width), slots),
            out_shape=(
                jax.ShapeDtypeStruct((rows,), jnp.float32),
                jax.ShapeDtypeStruct((rows, width), jnp.bfloat16),
                jax.ShapeDtypeStruct((rows, width), jnp.bfloat16),
            ),
            in_specs=[anywhere] * len(operands),
            out_specs=(vmem, vmem, vmem),
            scratch_shapes=[
                pltpu.VMEM((dp * head.shape[0], width), jnp.bfloat16),
                pltpu.VMEM((group, width), jnp.bfloat16),
                pltpu.VMEM((group, width), jnp.bfloat16),
                pltpu.VMEM((group, width), jnp.bfloat16),
                pltpu.SemaphoreType.DMA((len(operands),)),
            ],
            compiler_params=pltpu.CompilerParams(vmem_limit_bytes=40 * 1024 * 1024),
            name="group_softmax",
        )(*operands)

    return jax.shard_map(
        local,
        mesh=mesh,
        in_specs=(P(("dp", "rep"), None), P(("dp", "rep"), None), P("dp", None)),
        out_specs=(P(("dp", "rep")), P(("dp", "rep"), None), P(("dp", "rep"), None)),
        check_vma=False,
    )
```
